32 devices in a mesh: sect: 2 (over x), dp: 4 (over z), tp: 4 (over y, core).
Axes of the slice: x: 2, y: 2, z: 4, core: 2. Of those that a mesh axis runs over, the one named last changes fastest.
Arguments:
- w_key: bfloat16 [8192, 1024], P(('sect', 'dp', 'tp')), may hold values from -0.0625 to 0.0625
- w_value: bfloat16 [8192, 1024], P(('sect', 'dp', 'tp')), may hold values from -0.0625 to 0.0625
- hidden: bfloat16 [32, 16, 8192], P(('sect', 'dp'), None, 'tp'), may hold values from -6 to 6
- queries: bfloat16 [32, 16, 8192], P(('sect', 'dp'), None, 'tp'), may hold values from -36 to 36
- key_cache: bfloat16 [32, 512, 1024], P(('sect', 'dp'), None, 'tp'), may hold values from -6 to 6
- value_cache: bfloat16 [32, 512, 1024], P(('sect', 'dp'), None, 'tp'), may hold values from -6 to 6
- prompt_lengths: int32 [32], P(('sect', 'dp')), may hold values from 64 to 512
- rollout_lengths: int32 [32], P(('sect', 'dp')), may hold values from 1 to 16
- batch_slots: int32 [32], replicated, may hold values from 0 to 31, as said below
Outputs:
- batched: bfloat16 [32, 16, 8192], P(('sect', 'dp'), None, 'tp')
The draws below stay inside these ranges and needn't reach their ends.
Inputs may be any that keep to these rules, and one draw needn't show every extreme that they name: `batch_slots`: every row number appears once; a holder owns 4 consecutive rows of the micro-batch order, and the 4 sequences of one index of sect and dp go to 4 different holders.
All inputs are finite; a program needn't handle non-finite values.
Results may differ from the reference program's by a relative error of at most 0.0059.
Values may be sent and summed in bfloat16 or wider, within the bound.
No kernel may reach another device: no remote copies, remote signals or barrier semaphores. Data moves between devices by JAX's collectives and lax.ppermute only.
A program may use at most 64 MiB of HBM per device.

```python
import math
import jax
import jax.numpy as jnp
from jax import lax

D = 8192
QH = 64
KVH = 8
HEAD = 128
STEPS = 16
SEQ_DEV = 4
CTX = 512
SEQS = 32
KVW = 1024
GROUP = 8


def planting(key):
    signs = jax.random.randint(jax.random.fold_in(key, 11), (SEQS, HEAD), 0, 2).astype(jnp.float32) * 2.0 - 1.0
    heads = jax.random.randint(jax.random.fold_in(key, 12), (SEQS,), 0, QH)
    slots = jax.random.randint(jax.random.fold_in(key, 13), (SEQS,), 0, CTX // 8 - 1)
    dropped = jax.random.randint(jax.random.fold_in(key, 14), (SEQS,), 0, HEAD)
    levels = jax.random.randint(jax.random.fold_in(key, 15), (SEQS,), 0, 4)
    return (signs, heads, slots, dropped, levels)


def draw_key_cache(key, part):
    signs, heads, slots, dropped, levels = planting(key)
    key = jax.random.fold_in(key, 3)
    base = jnp.clip(jax.random.normal(key, (SEQS, CTX, KVW), jnp.float32), -6.0, 6.0)
    columns = jnp.arange(KVW)
    within = columns % HEAD
    in_head = (columns // HEAD)[None, :] == (heads // GROUP)[:, None]
    first = signs[:, within]
    second = jnp.where(within[None, :] == dropped[:, None], 0.0, first)
    rows = jnp.arange(CTX)
    first_row = rows[None, :] == slots[:, None]
    second_row = rows[None, :] == slots[:, None] + 1
    planted = jnp.where(first_row[:, :, None], first[:, None, :], second[:, None, :])
    chosen = in_head[:, None, :] & (first_row | second_row)[:, :, None]
    return jnp.where(chosen, planted, base).astype(jnp.bfloat16)


def draw_queries(key, part):
    signs, heads, slots, dropped, levels = planting(key)
    key = jax.random.fold_in(key, 5)
    shape = (SEQS, STEPS, QH * HEAD)
    base = jnp.clip(2.0 * jax.random.normal(key, shape, jnp.float32), -12.0, 12.0)
    strength = jnp.where(levels == 0, 1.1, jnp.where(levels == 1, 1.8, jnp.where(levels == 2, 2.5, 2.9))) * math.sqrt(HEAD)
    columns = jnp.arange(QH * HEAD)
    planted = signs[:, columns % HEAD] * strength[:, None]
    in_head = (columns // HEAD)[None, :] == heads[:, None]
    first_step = jnp.arange(STEPS) == 0
    chosen = in_head[:, None, :] & first_step[None, :, None]
    return jnp.where(chosen, planted[:, None, :], base).astype(jnp.bfloat16)


def draw_batch_slots(key, part):
    key = jax.random.fold_in(key, 7)
    holders_all = SEQS // SEQ_DEV
    order_key, shift_key, offset_key, place_key = jax.random.split(key, 4)
    sigma = jax.random.permutation(order_key, holders_all)
    tau = jax.random.permutation(shift_key, holders_all)
    offsets = jax.random.permutation(offset_key, holders_all)[:SEQ_DEV]
    holder = sigma[(tau[:, None] + offsets[None, :]) % holders_all]
    place_keys = jax.random.split(place_key, holders_all)
    places = jax.vmap(lambda k: jax.random.permutation(k, SEQ_DEV))(place_keys)
    within = places[holder, jnp.arange(SEQ_DEV)[None, :]]
    return (holder * SEQ_DEV + within).reshape(SEQS).astype(jnp.int32)


def plant(entries, own_key, smallest, high):
    longest = entries.shape.index(max(entries.shape))
    spots = []
    for shift in (0, 1):
        where = [jax.random.randint(jax.random.fold_in(own_key, axis), (), 0, length) for axis, length in enumerate(entries.shape)]
        where[longest] = (where[longest] + shift) % entries.shape[longest]
        spots.append(tuple(where))
    return entries.at[spots[0]].set(smallest).at[spots[1]].set(high)


def steps_of(rng, extent, pieces, low, top_value):
    def one(dim, parts):
        steps = jax.random.uniform(jax.random.fold_in(jax.random.fold_in(rng, 6), dim), (parts,), jnp.float32, low / len(pieces), top_value / len(pieces))
        return jnp.repeat(jnp.exp(steps), extent[dim] // parts).reshape((-1,) + (1,) * (len(extent) - dim - 1))

    gain = one(*pieces[0])
    for cut in pieces[1:]:
        gain = gain * one(*cut)
    return gain


def centred(stream_key, extent, spread, reach, shards=(), held_as=jnp.bfloat16):
    values = spread * jax.random.normal(stream_key, extent, jnp.float32)
    if shards:
        values = values * steps_of(stream_key, extent, shards, -0.22, 0.18)
    return jnp.clip(values, -reach, reach).astype(held_as)


def setup_inputs(seed: int = 0) -> dict:
    streams_of = jax.random.split(jax.random.key(seed), 10)
    return {
        "w_key": centred(streams_of[0], (D, KVW), D ** -0.5, 0.0625, ((0, 32),)),
        "w_value": centred(streams_of[1], (D, KVW), D ** -0.5, 0.0625, ((0, 32),)),
        "hidden": centred(streams_of[2], (SEQS, STEPS, D), 1.0, 6.0, ((0, 8), (2, 4))),
        "queries": draw_queries(jax.random.fold_in(streams_of[9], 71), 0),
        "key_cache": draw_key_cache(jax.random.fold_in(streams_of[9], 71), 0),
        "value_cache": centred(streams_of[5], (SEQS, CTX, KVW), 1.0, 6.0, ((0, 8), (2, 4))),
        "prompt_lengths": plant(jax.random.randint(streams_of[6], (SEQS,), CTX // 8, CTX + 1), jax.random.fold_in(streams_of[6], 1), CTX // 8, CTX).astype(jnp.int32),
        "rollout_lengths": plant(jax.random.randint(streams_of[7], (SEQS,), 1, STEPS + 1), jax.random.fold_in(streams_of[7], 1), 1, STEPS).astype(jnp.int32),
        "batch_slots": draw_batch_slots(jax.random.fold_in(streams_of[9], 71), 0),
    }


def attend(queries, new_keys, new_values, key_cache, value_cache, prompt_lengths, rollout_lengths):
    count = queries.shape[0]
    scale = HEAD ** -0.5
    query = queries.astype(jnp.float32).reshape(count, STEPS, KVH, GROUP, HEAD)
    cache_k = key_cache.astype(jnp.float32).reshape(count, CTX, KVH, HEAD)
    cache_v = value_cache.astype(jnp.float32).reshape(count, CTX, KVH, HEAD)
    fresh_k = new_keys.astype(jnp.float32).reshape(count, STEPS, KVH, HEAD)
    fresh_v = new_values.astype(jnp.float32).reshape(count, STEPS, KVH, HEAD)
    live = (jnp.arange(CTX)[None, :] < prompt_lengths[:, None])[:, None, None, None, :]
    causal = (jnp.arange(STEPS)[None, :] <= jnp.arange(STEPS)[:, None])[None, :, None, None, :]
    score_c = jnp.einsum("nikgd,njkd->nikgj", query, cache_k) * scale
    score_n = jnp.einsum("nikgd,njkd->nikgj", query, fresh_k) * scale
    score_c = jnp.where(live, score_c, -1e30)
    score_n = jnp.where(causal, score_n, -1e30)
    top = jnp.maximum(jnp.max(score_c, axis=-1), jnp.max(score_n, axis=-1))
    exp_c = jnp.exp(score_c - top[..., None])
    exp_n = jnp.exp(score_n - top[..., None])
    total = jnp.sum(exp_c, axis=-1) + jnp.sum(exp_n, axis=-1)
    weight_c = (exp_c / total[..., None]).astype(jnp.bfloat16).astype(jnp.float32)
    weight_n = (exp_n / total[..., None]).astype(jnp.bfloat16).astype(jnp.float32)
    result = jnp.einsum("nikgj,njkd->nikgd", weight_c, cache_v) + jnp.einsum("nikgj,njkd->nikgd", weight_n, fresh_v)
    keep = (jnp.arange(STEPS)[None, :] < rollout_lengths[:, None])[:, :, None, None, None]
    result = jnp.where(keep, result, 0.0)
    return result.astype(jnp.bfloat16).reshape(count, STEPS, QH * HEAD)


def reference(w_key, w_value, hidden, queries, key_cache, value_cache, prompt_lengths, rollout_lengths, batch_slots):
    flat = hidden.reshape(SEQS * STEPS, D)
    new_keys = jnp.dot(flat, w_key, preferred_element_type=jnp.float32).astype(jnp.bfloat16).reshape(SEQS, STEPS, KVW)
    new_values = jnp.dot(flat, w_value, preferred_element_type=jnp.float32).astype(jnp.bfloat16).reshape(SEQS, STEPS, KVW)
    blocks = SEQS // 8

    def split(a):
        return a.reshape((blocks, 8) + a.shape[1:])

    def one_block(items):
        return attend(*items)

    attended = lax.map(one_block, (split(queries), split(new_keys), split(new_values), split(key_cache), split(value_cache), split(prompt_lengths), split(rollout_lengths)))
    attended = attended.reshape(SEQS, STEPS, QH * HEAD)
    return jnp.zeros_like(attended).at[batch_slots].set(attended)
```

```python
import functools
import jax
import jax.numpy as jnp
from jax import lax
from jax.experimental import pallas as pl
from jax.experimental.pallas import tpu as pltpu
from jax.sharding import PartitionSpec as P

HEAD = 128
GROUP = 8
SCALE = HEAD ** (-0.5)
MIB = 1 << 20
CORE, HALF, SECT, DEPTH, PROMPT = range(5)


def vmem():
    return pl.BlockSpec(memory_space=pltpu.VMEM)


def smem():
    return pl.BlockSpec(memory_space=pltpu.SMEM)


def limit(*arrays):
    total = sum(a.size * a.dtype.itemsize for a in arrays)
    return pltpu.CompilerParams(vmem_limit_bytes=max(6 * MIB, total + 2 * MIB))


def stacked_heads(q, kv):
    first = kv * GROUP
    return jnp.concatenate(
        [q[:, (first + g) * HEAD : (first + g + 1) * HEAD] for g in range(GROUP)], axis=0
    )


def dot32(a, b):
    return jnp.dot(a, b, preferred_element_type=jnp.float32)


def dot_t(a, b):
    return lax.dot_general(a, b, (((1,), (1,)), ((), ())), preferred_element_type=jnp.float32)


def bf16(a):
    return a.astype(jnp.bfloat16)


def cache_kernel(meta_ref, q_ref, k_ref, v_ref, o_ref, stat_ref):
    slots, width = k_ref.shape[1:]
    steps = q_ref.shape[1]
    rows = steps * GROUP
    live = lax.broadcasted_iota(jnp.int32, (rows, slots), 1) < meta_ref[PROMPT + pl.program_id(0)]
    lane = lax.broadcasted_iota(jnp.int32, (rows, HEAD), 1)
    for kv in range(width // HEAD):
        cols = slice(kv * HEAD, (kv + 1) * HEAD)
        q = stacked_heads(q_ref[0], kv)
        s = jnp.where(live, dot_t(q, k_ref[0, :, cols]) * SCALE, -1e30)
        top = jnp.max(s, axis=1, keepdims=True)
        e = jnp.exp(s - top)
        total = jnp.sum(e, axis=1, keepdims=True)
        o_ref[0, kv] = dot32(bf16(e), v_ref[0, :, cols])
        stat_ref[0, kv] = jnp.where(lane == 0, top, total)


def cache_attention(meta, queries, key_cache, value_cache):
    count, steps, qw = queries.shape
    slots, width = key_cache.shape[1:]
    shape = (count, width // HEAD, steps * GROUP, HEAD)

    def one(n, meta):
        return (n, 0, 0)

    def one4(n, meta):
        return (n, 0, 0, 0)

    return pl.pallas_call(
        cache_kernel,
        grid_spec=pltpu.PrefetchScalarGridSpec(
            num_scalar_prefetch=1,
            grid=(count,),
            in_specs=[
                pl.BlockSpec((1, steps, qw), one),
                pl.BlockSpec((1, slots, width), one),
                pl.BlockSpec((1, slots, width), one),
            ],
            out_specs=[pl.BlockSpec((1,) + shape[1:], one4)] * 2,
        ),
        out_shape=[jax.ShapeDtypeStruct(shape, jnp.float32)] * 2,
        compiler_params=pltpu.CompilerParams(vmem_limit_bytes=8 * MIB),
        name="cache_attention",
    )(meta, queries, key_cache, value_cache)


def project_kernel(dp, meta_ref, x_ref, key_ref, value_ref, key_mate_ref, value_mate_ref, *refs):
    out_refs, w_ref, held = refs[:8], refs[8], refs[9]
    seqs, steps, width = held.shape
    count = seqs // dp
    rows, kind_width = key_ref.shape
    core, half = meta_ref[CORE], meta_ref[HALF]
    for side, pair in ((0, (key_ref, value_ref)), (1, (key_mate_ref, value_mate_ref))):
        for kind, ref in enumerate(pair):
            first = pl.multiple_of((core ^ side) * rows, rows)
            w_ref[pl.ds(first, rows), kind * kind_width : (kind + 1) * kind_width] = ref[...]
    place = (meta_ref[DEPTH] & (dp // 2 - 1)) * 2 + half
    chunk = 4 * count * steps
    for m in range(dp):
        if m % 4 == 0:
            first = m * count * steps
            sums = bf16(dot32(x_ref[first : first + chunk], w_ref[...]))
        for n in range(count):
            i = (m % 4) * count + n
            held[(place ^ m) * count + n] = sums[i * steps : (i + 1) * steps]
    cw = width // 8
    own_half = (meta_ref[DEPTH] >= dp // 2).astype(jnp.int32)
    for i, ref in enumerate(out_refs):
        t = (half ^ ((i >> 1) & 1)) * 2 + (meta_ref[SECT] ^ (i & 1))
        group = pl.ds((own_half ^ (1 - (i >> 2))) * (seqs // 2), seqs // 2)
        for kind in range(2):
            cols = pl.ds(pl.multiple_of(kind * kind_width + t * cw, cw), cw)
            ref[:, :, kind * cw : (kind + 1) * cw] = held[group, :, cols]


def project(meta, x, weights, mates, dp, steps):
    seqs = x.shape[0] // steps
    rows, width = weights[0].shape
    out = jax.ShapeDtypeStruct((seqs // 2, steps, width // 2), jnp.bfloat16)
    return pl.pallas_call(
        functools.partial(project_kernel, dp),
        in_specs=[smem()] + [vmem()] * 5,
        out_specs=[vmem()] * 8,
        out_shape=[out] * 8,
        scratch_shapes=[
            pltpu.VMEM((2 * rows, 2 * width), x.dtype),
            pltpu.VMEM((seqs, steps, 2 * width), jnp.bfloat16),
        ],
        compiler_params=limit(x, *weights, *weights, *weights, *weights, *[out] * 32),
        name="project",
    )(meta, x, *weights, *mates)


def cut_kernel(spans, meta_ref, *refs):
    in_refs, out_refs = refs[:-spans], refs[-spans:]
    count = out_refs[0].shape[0]
    place = meta_ref[DEPTH] & (spans - 1)
    for m, ref in enumerate(out_refs):
        rows = pl.ds((place ^ m) * count, count)
        total = in_refs[0][rows].astype(jnp.float32)
        for part in in_refs[1:]:
            total += part[rows].astype(jnp.float32)
        ref[...] = total.astype(ref.dtype)


def cut(meta, parts, spans, first_type):
    shape = (parts[0].shape[0] // spans,) + parts[0].shape[1:]
    return pl.pallas_call(
        functools.partial(cut_kernel, spans),
        in_specs=[smem()] + [vmem()] * len(parts),
        out_specs=[vmem()] * spans,
        out_shape=[jax.ShapeDtypeStruct(shape, first_type)]
        + [jax.ShapeDtypeStruct(shape, jnp.bfloat16)] * (spans - 1),
        compiler_params=limit(*parts, *parts, *parts),
        name="cut",
    )(meta, *parts)


def own_group(meta_ref, groups):
    return meta_ref[SECT] * (groups // 2) + meta_ref[DEPTH]


def merge_kernel(groups, meta_ref, q_ref, o_ref, stat_ref, *refs):
    part_refs, out_refs, held = refs[: -groups - 1], refs[-groups - 1 : -1], refs[-1]
    count, steps, _ = q_ref.shape
    width = part_refs[0].shape[2] // 2
    rows = steps * GROUP
    fresh = part_refs[0][...]
    for ref in part_refs[1:]:
        fresh += ref[...].astype(jnp.float32)
    fresh = bf16(fresh).reshape(count * steps, 2 * width)
    shape = (count * rows, count * steps)
    row = lax.broadcasted_iota(jnp.int32, shape, 0)
    col = lax.broadcasted_iota(jnp.int32, shape, 1)
    causal = (row // rows == col // steps) & (col % steps <= row % steps)
    step = lax.broadcasted_iota(jnp.int32, (rows, HEAD), 0) % steps
    keep = jnp.concatenate([step < meta_ref[PROMPT + count + n] for n in range(count)], axis=0)
    for kv in range(width // HEAD):
        q = jnp.concatenate([stacked_heads(q_ref[n], kv) for n in range(count)], axis=0)
        stat = jnp.concatenate([stat_ref[n, kv, :, :2] for n in range(count)], axis=0)
        o = jnp.concatenate([o_ref[n, kv] for n in range(count)], axis=0)
        k = fresh[:, kv * HEAD : (kv + 1) * HEAD]
        v = fresh[:, width + kv * HEAD : width + (kv + 1) * HEAD]
        s = jnp.where(causal, dot_t(q, k) * SCALE, -1e30)
        top = jnp.maximum(stat[:, :1], jnp.max(s, axis=1, keepdims=True))
        e = jnp.exp(s - top)
        back = jnp.exp(stat[:, :1] - top)
        share = 1.0 / (back * stat[:, 1:] + jnp.sum(e, axis=1, keepdims=True))
        r = o * (back * share) + dot32(bf16(e * share), v)
        r = bf16(jnp.where(keep, r, 0.0))
        for n in range(count):
            for g in range(GROUP):
                h = kv * GROUP + g
                first = n * rows + g * steps
                held[n, :, h * HEAD : (h + 1) * HEAD] = r[first : first + steps]
    own = own_group(meta_ref, groups)
    slots = PROMPT + 2 * count
    for n in range(count):
        holder = lax.div(meta_ref[slots + own * count + n], count)
        for i in range(groups):

            @pl.when((holder ^ own) == i)
            def _():
                out_refs[i][...] = held[n]


def merge(meta, queries, o_cache, stats, parts, groups):
    shape = queries.shape[1:]
    return pl.pallas_call(
        functools.partial(merge_kernel, groups),
        in_specs=[smem()] + [vmem()] * (3 + len(parts)),
        out_specs=[vmem()] * groups,
        out_shape=[jax.ShapeDtypeStruct(shape, jnp.bfloat16)] * groups,
        scratch_shapes=[pltpu.VMEM(queries.shape, jnp.bfloat16)],
        compiler_params=limit(queries, o_cache, stats, *parts, *[queries] * (groups // queries.shape[0] + 1)),
        name="merge_fresh",
    )(meta, queries, o_cache, stats, *parts)


def pick_kernel(order, meta_ref, *refs):
    in_refs, out_ref, places = refs[:-2], refs[-2], refs[-1]
    groups = len(in_refs)
    count = out_ref.shape[0]
    slots = PROMPT + 2 * count

    def note(s, carry):
        places[meta_ref[slots + s]] = s
        return carry

    lax.fori_loop(0, groups * count, note, 0, unroll=8)
    own = own_group(meta_ref, groups)
    for r in range(count):
        source = lax.div(places[own * count + r], count)
        for m, ref in zip(order, in_refs):

            @pl.when((source ^ own) == m)
            def _():
                out_ref[r] = ref[...]


def pick(meta, blocks, order, count):
    out = jax.ShapeDtypeStruct((count,) + blocks[0].shape, jnp.bfloat16)
    return pl.pallas_call(
        functools.partial(pick_kernel, order),
        in_specs=[smem()] + [vmem()] * len(blocks),
        out_specs=vmem(),
        out_shape=out,
        scratch_shapes=[pltpu.SMEM((len(blocks) * count,), jnp.int32)],
        compiler_params=limit(out, *blocks),
        name="pick_rows",
    )(meta, *blocks)


def shards(
    dp,
    w_key,
    w_value,
    hidden,
    queries,
    key_cache,
    value_cache,
    prompt_lengths,
    rollout_lengths,
    batch_slots,
):
    count, steps, feats = hidden.shape
    tokens = count * steps
    groups = 2 * dp
    spans = dp // 2
    wide = feats // dp
    x, z, t = lax.axis_index("sect"), lax.axis_index("dp"), lax.axis_index("tp")
    p, c = t >> 1, t & 1
    everyone = ("sect", "dp", "tp")
    devices = [(i, j, k) for i in range(2) for j in range(dp) for k in range(4)]

    def flat(i, j, k):
        return (i * dp + j) * 4 + k

    def send(a, target):
        return lax.ppermute(a, everyone, [(flat(*d), target(*d)) for d in devices])

    def to_features(m):
        def target(i, j, k):
            e, half = divmod(j ^ m, 2)
            return (k * spans + e) * 4 + half * 2 + i

        return target

    def to_mate(i, j, k):
        return flat(i, j, k ^ 1)

    def in_plane(m):
        return lambda i, j, k: flat(k & 1, j, ((k >> 1) ^ (m >> 1)) * 2 + (i ^ (m & 1)))

    def to_depth(m):
        return lambda i, j, k: flat(i, j ^ m, k)

    def to_group(m):
        return lambda i, j, k: ((i * dp + j) ^ m) * 4 + k

    scalars = jnp.stack([c, p, x, z]).astype(jnp.int32)
    meta = jnp.concatenate([scalars, prompt_lengths, rollout_lengths, batch_slots])

    flat_hidden = hidden.reshape(tokens, feats)
    near = [
        send(lax.dynamic_slice_in_dim(flat_hidden, (z ^ m) * wide, wide, 1), to_features(m))
        for m in range(dp)
    ]
    weights = (w_key, w_value)
    mates = [send(w, to_mate) for w in weights]
    o_cache, stats = cache_attention(meta, queries, key_cache, value_cache)

    parts = project(meta, jnp.concatenate(near, axis=0), weights, mates, dp, steps)
    far, near = ([send(parts[first + m], in_plane(m)) for m in (3, 2, 1, 0)] for first in (0, 4))
    far = cut(meta, far, spans, jnp.bfloat16)
    far = [send(a, to_depth(spans + m)) for m, a in enumerate(far)]
    near = cut(meta, near, spans, jnp.float32)
    near = [a if m == 0 else send(a, to_depth(m)) for m, a in enumerate(near)]
    parts = near + far
    sends = merge(meta, queries, o_cache, stats, parts, groups)
    order = sorted(range(1, groups), key=lambda m: -(m & (dp - 1)))
    blocks = [send(sends[m], to_group(m)) for m in order]
    return pick(meta, blocks + [sends[0]], order + [0], count)


def solution(mesh):
    in_specs = (
        P(("sect", "dp", "tp"), None),
        P(("sect", "dp", "tp"), None),
        P(("sect", "dp"), None, "tp"),
        P(("sect", "dp"), None, "tp"),
        P(("sect", "dp"), None, "tp"),
        P(("sect", "dp"), None, "tp"),
        P(("sect", "dp")),
        P(("sect", "dp")),
        P(),
    )
    out_specs = P(("sect", "dp"), None, "tp")
    body = functools.partial(shards, mesh.shape["dp"])
    return jax.shard_map(body, mesh=mesh, in_specs=in_specs, out_specs=out_specs, check_vma=False)
```

```python
import functools
import jax
import jax.numpy as jnp
from jax import lax
from jax.experimental import pallas as pl
from jax.experimental.pallas import tpu as pltpu
from jax.sharding import PartitionSpec as P

HEAD = 128
GROUP = 8
SCALE = HEAD ** (-0.5)
MIB = 1 << 20
CORE, HALF, SECT, DEPTH, PROMPT = range(5)


def vmem():
    return pl.BlockSpec(memory_space=pltpu.VMEM)


def smem():
    return pl.BlockSpec(memory_space=pltpu.SMEM)


def limit(*arrays):
    total = sum(a.size * a.dtype.itemsize for a in arrays)
    return pltpu.CompilerParams(vmem_limit_bytes=max(6 * MIB, total + 2 * MIB))


def stacked_heads(q, kv):
    first = kv * GROUP
    return jnp.concatenate(
        [q[:, (first + g) * HEAD : (first + g + 1) * HEAD] for g in range(GROUP)], axis=0
    )


def dot32(a, b):
    return jnp.dot(a, b, preferred_element_type=jnp.float32)


def dot_t(a, b):
    return lax.dot_general(a, b, (((1,), (1,)), ((), ())), preferred_element_type=jnp.float32)


def bf16(a):
    return a.astype(jnp.bfloat16)


def cache_kernel(meta_ref, q_ref, k_ref, v_ref, o_ref, stat_ref):
    slots, width = k_ref.shape[1:]
    steps = q_ref.shape[1]
    rows = steps * GROUP
    live = lax.broadcasted_iota(jnp.int32, (rows, slots), 1) < meta_ref[PROMPT + pl.program_id(0)]
    lane = lax.broadcasted_iota(jnp.int32, (rows, HEAD), 1)
    for kv in range(width // HEAD):
        cols = slice(kv * HEAD, (kv + 1) * HEAD)
        q = stacked_heads(q_ref[0], kv)
        s = jnp.where(live, dot_t(q, k_ref[0, :, cols]) * SCALE, -1e30)
        top = jnp.max(s, axis=1, keepdims=True)
        e = jnp.exp(s - top)
        total = jnp.sum(e, axis=1, keepdims=True)
        o_ref[0, kv] = dot32(bf16(e), v_ref[0, :, cols])
        stat_ref[0, kv] = jnp.where(lane == 0, top, total)


def cache_attention(meta, queries, key_cache, value_cache):
    count, steps, qw = queries.shape
    slots, width = key_cache.shape[1:]
    shape = (count, width // HEAD, steps * GROUP, HEAD)

    def one(n, meta):
        return (n, 0, 0)

    def one4(n, meta):
        return (n, 0, 0, 0)

    return pl.pallas_call(
        cache_kernel,
        grid_spec=pltpu.PrefetchScalarGridSpec(
            num_scalar_prefetch=1,
            grid=(count,),
            in_specs=[
                pl.BlockSpec((1, steps, qw), one),
                pl.BlockSpec((1, slots, width), one),
                pl.BlockSpec((1, slots, width), one),
            ],
            out_specs=[pl.BlockSpec((1,) + shape[1:], one4)] * 2,
        ),
        out_shape=[jax.ShapeDtypeStruct(shape, jnp.float32)] * 2,
        compiler_params=pltpu.CompilerParams(vmem_limit_bytes=8 * MIB),
        name="cache_attention",
    )(meta, queries, key_cache, value_cache)


def project_kernel(dp, meta_ref, x_ref, key_ref, value_ref, key_mate_ref, value_mate_ref, *refs):
    out_refs, held = refs[:8], refs[8]
    seqs, steps, width = held.shape
    count = seqs // dp
    rows, kind_width = key_ref.shape
    core, half = meta_ref[CORE], meta_ref[HALF]
    first, second = x_ref[:, :rows], x_ref[:, rows:]
    own, mate = jnp.where(core == 0, first, second), jnp.where(core == 0, second, first)
    place = (meta_ref[DEPTH] & (dp // 2 - 1)) * 2 + half
    chunk = 4 * count * steps
    for kind, refs in enumerate(((key_ref, key_mate_ref), (value_ref, value_mate_ref))):
        cols = slice(kind * kind_width, (kind + 1) * kind_width)
        for m in range(dp):
            if m % 4 == 0:
                part = slice(m * count * steps, m * count * steps + chunk)
                sums = bf16(dot32(own[part], refs[0][...]) + dot32(mate[part], refs[1][...]))
            for n in range(count):
                i = (m % 4) * count + n
                held[(place ^ m) * count + n, :, cols] = sums[i * steps : (i + 1) * steps]
    cw = width // 8
    own_half = (meta_ref[DEPTH] >= dp // 2).astype(jnp.int32)
    for i, ref in enumerate(out_refs):
        t = (half ^ ((i >> 1) & 1)) * 2 + (meta_ref[SECT] ^ (i & 1))
        group = pl.ds((own_half ^ (1 - (i >> 2))) * (seqs // 2), seqs // 2)
        for kind in range(2):
            cols = pl.ds(pl.multiple_of(kind * kind_width + t * cw, cw), cw)
            ref[:, :, kind * cw : (kind + 1) * cw] = held[group, :, cols]


def project(meta, x, weights, mates, dp, steps):
    seqs = x.shape[0] // steps
    rows, width = weights[0].shape
    out = jax.ShapeDtypeStruct((seqs // 2, steps, width // 2), jnp.bfloat16)
    return pl.pallas_call(
        functools.partial(project_kernel, dp),
        in_specs=[smem()] + [vmem()] * 5,
        out_specs=[vmem()] * 8,
        out_shape=[out] * 8,
        scratch_shapes=[pltpu.VMEM((seqs, steps, 2 * width), jnp.bfloat16)],
        compiler_params=limit(x, *weights, *weights, *weights, *weights, *[out] * 32),
        name="project",
    )(meta, x, *weights, *mates)


def add_kernel(*refs):
    total = refs[0][...].astype(jnp.float32)
    for ref in refs[1:-1]:
        total += ref[...].astype(jnp.float32)
    refs[-1][...] = bf16(total)


def add(parts):
    out = jax.ShapeDtypeStruct(parts[0].shape, jnp.bfloat16)
    return pl.pallas_call(
        add_kernel,
        in_specs=[vmem()] * len(parts),
        out_specs=vmem(),
        out_shape=out,
        compiler_params=limit(out, out, out, *parts),
        name="add",
    )(*parts)


def cut_kernel(spans, meta_ref, _, *refs):
    in_refs, out_refs = refs[:-spans], refs[-spans:]
    count = out_refs[0].shape[0]
    place = meta_ref[DEPTH] & (spans - 1)
    for m, ref in enumerate(out_refs):
        rows = pl.ds((place ^ m) * count, count)
        total = in_refs[0][rows].astype(jnp.float32)
        for part in in_refs[1:]:
            total += part[rows].astype(jnp.float32)
        ref[...] = total.astype(ref.dtype)


def cut(meta, before, parts, spans):
    shape = (parts[0].shape[0] // spans,) + parts[0].shape[1:]
    return pl.pallas_call(
        functools.partial(cut_kernel, spans),
        in_specs=[smem()] + [vmem()] * (1 + len(parts)),
        out_specs=[vmem()] * spans,
        out_shape=[jax.ShapeDtypeStruct(shape, jnp.float32)]
        + [jax.ShapeDtypeStruct(shape, jnp.bfloat16)] * (spans - 1),
        compiler_params=limit(before, *parts, *parts, *parts),
        name="cut",
    )(meta, before, *parts)


def own_group(meta_ref, groups):
    return meta_ref[SECT] * (groups // 2) + meta_ref[DEPTH]


def merge_kernel(groups, meta_ref, q_ref, o_ref, stat_ref, *refs):
    part_refs, out_refs, held = refs[: -groups - 1], refs[-groups - 1 : -1], refs[-1]
    count, steps, _ = q_ref.shape
    width = part_refs[0].shape[2] // 2
    rows = steps * GROUP
    fresh = part_refs[0][...]
    for ref in part_refs[1:]:
        fresh += ref[...].astype(jnp.float32)
    fresh = bf16(fresh).reshape(count * steps, 2 * width)
    shape = (count * rows, count * steps)
    row = lax.broadcasted_iota(jnp.int32, shape, 0)
    col = lax.broadcasted_iota(jnp.int32, shape, 1)
    causal = (row // rows == col // steps) & (col % steps <= row % steps)
    step = lax.broadcasted_iota(jnp.int32, (rows, HEAD), 0) % steps
    keep = jnp.concatenate([step < meta_ref[PROMPT + count + n] for n in range(count)], axis=0)
    for kv in range(width // HEAD):
        q = jnp.concatenate([stacked_heads(q_ref[n], kv) for n in range(count)], axis=0)
        stat = jnp.concatenate([stat_ref[n, kv, :, :2] for n in range(count)], axis=0)
        o = jnp.concatenate([o_ref[n, kv] for n in range(count)], axis=0)
        k = fresh[:, kv * HEAD : (kv + 1) * HEAD]
        v = fresh[:, width + kv * HEAD : width + (kv + 1) * HEAD]
        s = jnp.where(causal, dot_t(q, k) * SCALE, -1e30)
        top = jnp.maximum(stat[:, :1], jnp.max(s, axis=1, keepdims=True))
        e = jnp.exp(s - top)
        back = jnp.exp(stat[:, :1] - top)
        share = 1.0 / (back * stat[:, 1:] + jnp.sum(e, axis=1, keepdims=True))
        r = o * (back * share) + dot32(bf16(e * share), v)
        r = bf16(jnp.where(keep, r, 0.0))
        for n in range(count):
            for g in range(GROUP):
                h = kv * GROUP + g
                first = n * rows + g * steps
                held[n, :, h * HEAD : (h + 1) * HEAD] = r[first : first + steps]
    own = own_group(meta_ref, groups)
    slots = PROMPT + 2 * count
    for n in range(count):
        holder = lax.div(meta_ref[slots + own * count + n], count)
        for i in range(groups):

            @pl.when((holder ^ own) == i)
            def _():
                out_refs[i][...] = held[n]


def merge(meta, queries, o_cache, stats, parts, groups):
    shape = queries.shape[1:]
    return pl.pallas_call(
        functools.partial(merge_kernel, groups),
        in_specs=[smem()] + [vmem()] * (3 + len(parts)),
        out_specs=[vmem()] * groups,
        out_shape=[jax.ShapeDtypeStruct(shape, jnp.bfloat16)] * groups,
        scratch_shapes=[pltpu.VMEM(queries.shape, jnp.bfloat16)],
        compiler_params=limit(queries, o_cache, stats, *parts, *[queries] * (groups // queries.shape[0] + 1)),
        name="merge_fresh",
    )(meta, queries, o_cache, stats, *parts)


def pick_kernel(order, meta_ref, *refs):
    in_refs, out_ref, places, sems = refs[:-3], refs[-3], refs[-2], refs[-1]
    groups = len(in_refs)
    count = out_ref.shape[0]
    slots = PROMPT + 2 * count

    def note(s, carry):
        places[meta_ref[slots + s]] = s
        return carry

    lax.fori_loop(0, groups * count, note, 0, unroll=8)
    own = own_group(meta_ref, groups)
    for r in range(count):
        source = lax.div(places[own * count + r], count)
        for m, ref in zip(order, in_refs):

            @pl.when((source ^ own) == m)
            def _():
                pltpu.make_async_copy(ref, out_ref.at[r], sems.at[r]).start()

    for r in range(count):
        pltpu.make_async_copy(in_refs[0], out_ref.at[r], sems.at[r]).wait()


def pick(meta, blocks, order, count):
    out = jax.ShapeDtypeStruct((count,) + blocks[0].shape, jnp.bfloat16)
    return pl.pallas_call(
        functools.partial(pick_kernel, order),
        in_specs=[smem()] + [vmem()] * len(blocks),
        out_specs=pl.BlockSpec(memory_space=pl.ANY),
        out_shape=out,
        scratch_shapes=[
            pltpu.SMEM((len(blocks) * count,), jnp.int32),
            pltpu.SemaphoreType.DMA((count,)),
        ],
        compiler_params=limit(*blocks),
        name="pick_rows",
    )(meta, *blocks)


def shards(
    dp,
    w_key,
    w_value,
    hidden,
    queries,
    key_cache,
    value_cache,
    prompt_lengths,
    rollout_lengths,
    batch_slots,
):
    count, steps, feats = hidden.shape
    tokens = count * steps
    groups = 2 * dp
    spans = dp // 2
    wide = feats // dp
    x, z, t = lax.axis_index("sect"), lax.axis_index("dp"), lax.axis_index("tp")
    p, c = t >> 1, t & 1
    everyone = ("sect", "dp", "tp")
    devices = [(i, j, k) for i in range(2) for j in range(dp) for k in range(4)]

    def flat(i, j, k):
        return (i * dp + j) * 4 + k

    def send(a, target):
        return lax.ppermute(a, everyone, [(flat(*d), target(*d)) for d in devices])

    def to_features(m):
        def target(i, j, k):
            e, half = divmod(j ^ m, 2)
            return (k * spans + e) * 4 + half * 2 + i

        return target

    def to_mate(i, j, k):
        return flat(i, j, k ^ 1)

    def in_plane(m):
        return lambda i, j, k: flat(k & 1, j, ((k >> 1) ^ (m >> 1)) * 2 + (i ^ (m & 1)))

    def to_depth(m):
        return lambda i, j, k: flat(i, j ^ m, k)

    def to_group(m):
        return lambda i, j, k: ((i * dp + j) ^ m) * 4 + k

    scalars = jnp.stack([c, p, x, z]).astype(jnp.int32)
    meta = jnp.concatenate([scalars, prompt_lengths, rollout_lengths, batch_slots])

    flat_hidden = hidden.reshape(tokens, feats)
    near = [
        send(lax.dynamic_slice_in_dim(flat_hidden, (z ^ m) * wide, wide, 1), to_features(m))
        for m in range(dp)
    ]
    weights = (w_key, w_value)
    mates = [send(w, to_mate) for w in weights]
    o_cache, stats = cache_attention(meta, queries, key_cache, value_cache)

    parts = project(meta, jnp.concatenate(near, axis=0), weights, mates, dp, steps)
    far, near = ([send(parts[first + m], in_plane(m)) for m in (3, 2, 1, 0)] for first in (0, 4))
    near = cut(meta, stats, near + [send(add(far), to_depth(spans))], spans)
    parts = [a if m == 0 else send(a, to_depth(m)) for m, a in enumerate(near)]
    sends = merge(meta, queries, o_cache, stats, parts, groups)
    order = sorted(range(1, groups), key=lambda m: -(m & (dp - 1)))
    blocks = [send(sends[m], to_group(m)) for m in order]
    return pick(meta, blocks + [sends[0]], order + [0], count)


def solution(mesh):
    in_specs = (
        P(("sect", "dp", "tp"), None),
        P(("sect", "dp", "tp"), None),
        P(("sect", "dp"), None, "tp"),
        P(("sect", "dp"), None, "tp"),
        P(("sect", "dp"), None, "tp"),
        P(("sect", "dp"), None, "tp"),
        P(("sect", "dp")),
        P(("sect", "dp")),
        P(),
    )
    out_specs = P(("sect", "dp"), None, "tp")
    body = functools.partial(shards, mesh.shape["dp"])
    return jax.shard_map(body, mesh=mesh, in_specs=in_specs, out_specs=out_specs, check_vma=False)
```

```python
import functools
import jax
import jax.numpy as jnp
from jax import lax
from jax.experimental import pallas as pl
from jax.experimental.pallas import tpu as pltpu
from jax.sharding import PartitionSpec as P

HEAD = 128
GROUP = 8
SCALE = HEAD ** (-0.5)
MIB = 1 << 20
SECT, DEPTH, PROMPT = range(3)


def vmem():
    return pl.BlockSpec(memory_space=pltpu.VMEM)


def smem():
    return pl.BlockSpec(memory_space=pltpu.SMEM)


def limit(*arrays):
    total = sum(a.size * a.dtype.itemsize for a in arrays)
    return pltpu.CompilerParams(vmem_limit_bytes=max(6 * MIB, total + 2 * MIB))


def stacked_heads(q, kv):
    first = kv * GROUP
    return jnp.concatenate(
        [q[:, (first + g) * HEAD : (first + g + 1) * HEAD] for g in range(GROUP)], axis=0
    )


def dot32(a, b):
    return jnp.dot(a, b, preferred_element_type=jnp.float32)


def dot_t(a, b):
    return lax.dot_general(a, b, (((1,), (1,)), ((), ())), preferred_element_type=jnp.float32)


def bf16(a):
    return a.astype(jnp.bfloat16)


def cache_kernel(groups, meta_ref, q_ref, k_ref, v_ref, o_ref, stat_ref, source_ref, places):
    count = source_ref.shape[0]

    @pl.when(pl.program_id(0) == 0)
    def _():
        def note(s, carry):
            places[meta_ref[PROMPT + 2 * count + s]] = s
            return carry

        lax.fori_loop(0, groups * count, note, 0, unroll=8)
        own = own_group(meta_ref, groups)
        for r in range(count):
            source = lax.div(places[own * count + r], count) ^ own
            source_ref[r] = bf16(jnp.full(source_ref.shape[1:], source.astype(jnp.float32)))

    slots, width = k_ref.shape[1:]
    steps = q_ref.shape[1]
    rows = steps * GROUP
    live = lax.broadcasted_iota(jnp.int32, (rows, slots), 1) < meta_ref[PROMPT + pl.program_id(0)]
    lane = lax.broadcasted_iota(jnp.int32, (rows, HEAD), 1)
    for kv in range(width // HEAD):
        cols = slice(kv * HEAD, (kv + 1) * HEAD)
        q = stacked_heads(q_ref[0], kv)
        s = jnp.where(live, dot_t(q, k_ref[0, :, cols]) * SCALE, -1e30)
        top = jnp.max(s, axis=1, keepdims=True)
        e = jnp.exp(s - top)
        total = jnp.sum(e, axis=1, keepdims=True)
        o_ref[0, kv] = dot32(bf16(e), v_ref[0, :, cols])
        stat_ref[0, kv] = jnp.where(lane == 0, top, total)


def cache_attention(meta, queries, key_cache, value_cache, groups):
    count, steps, qw = queries.shape
    slots, width = key_cache.shape[1:]
    shape = (count, width // HEAD, steps * GROUP, HEAD)

    def one(n, meta):
        return (n, 0, 0)

    def one4(n, meta):
        return (n, 0, 0, 0)

    return pl.pallas_call(
        functools.partial(cache_kernel, groups),
        grid_spec=pltpu.PrefetchScalarGridSpec(
            num_scalar_prefetch=1,
            grid=(count,),
            in_specs=[
                pl.BlockSpec((1, steps, qw), one),
                pl.BlockSpec((1, slots, width), one),
                pl.BlockSpec((1, slots, width), one),
            ],
            out_specs=[pl.BlockSpec((1,) + shape[1:], one4)] * 2
            + [pl.BlockSpec((count, steps, HEAD), lambda n, meta: (0, 0, 0))],
            scratch_shapes=[pltpu.SMEM((groups * count,), jnp.int32)],
        ),
        out_shape=[jax.ShapeDtypeStruct(shape, jnp.float32)] * 2
        + [jax.ShapeDtypeStruct((count, steps, HEAD), jnp.bfloat16)],
        compiler_params=pltpu.CompilerParams(vmem_limit_bytes=8 * MIB),
        name="cache_attention",
    )(meta, queries, key_cache, value_cache)


def project_kernel(dp, x_ref, key_ref, value_ref, key_mate_ref, value_mate_ref, *refs):
    out_refs, held = refs[:8], refs[8]
    seqs, steps, width = held.shape
    count = seqs // dp
    rows, kind_width = key_ref.shape
    core, half = lax.axis_index("tp") & 1, lax.axis_index("tp") >> 1
    sect, depth = lax.axis_index("sect"), lax.axis_index("dp")
    first, second = x_ref[:, :rows], x_ref[:, rows:]
    own, mate = jnp.where(core == 0, first, second), jnp.where(core == 0, second, first)
    place = (depth & (dp // 2 - 1)) * 2 + half
    chunk = 4 * count * steps
    for kind, refs in enumerate(((key_ref, key_mate_ref), (value_ref, value_mate_ref))):
        cols = slice(kind * kind_width, (kind + 1) * kind_width)
        for m in range(dp):
            if m % 4 == 0:
                part = slice(m * count * steps, m * count * steps + chunk)
                sums = bf16(dot32(own[part], refs[0][...]) + dot32(mate[part], refs[1][...]))
            for n in range(count):
                i = (m % 4) * count + n
                held[(place ^ m) * count + n, :, cols] = sums[i * steps : (i + 1) * steps]
    cw = width // 8
    own_half = (depth >= dp // 2).astype(jnp.int32)
    for i, ref in enumerate(out_refs):
        t = (half ^ ((i >> 1) & 1)) * 2 + (sect ^ (i & 1))
        group = pl.ds((own_half ^ (1 - (i >> 2))) * (seqs // 2), seqs // 2)
        for kind in range(2):
            cols = pl.ds(pl.multiple_of(kind * kind_width + t * cw, cw), cw)
            ref[:, :, kind * cw : (kind + 1) * cw] = held[group, :, cols]


def project(x, weights, mates, dp, steps):
    seqs = x.shape[0] // steps
    rows, width = weights[0].shape
    out = jax.ShapeDtypeStruct((seqs // 2, steps, width // 2), jnp.bfloat16)
    return pl.pallas_call(
        functools.partial(project_kernel, dp),
        in_specs=[vmem()] * 5,
        out_specs=[vmem()] * 8,
        out_shape=[out] * 8,
        scratch_shapes=[pltpu.VMEM((seqs, steps, 2 * width), jnp.bfloat16)],
        compiler_params=limit(x, *weights, *weights, *weights, *weights, *[out] * 32),
        name="project",
    )(x, *weights, *mates)


def add_kernel(*refs):
    total = refs[0][...].astype(jnp.float32)
    for ref in refs[1:-1]:
        total += ref[...].astype(jnp.float32)
    refs[-1][...] = bf16(total)


def add(parts):
    out = jax.ShapeDtypeStruct(parts[0].shape, jnp.bfloat16)
    return pl.pallas_call(
        add_kernel,
        in_specs=[vmem()] * len(parts),
        out_specs=vmem(),
        out_shape=out,
        compiler_params=limit(out, out, out, *parts),
        name="add",
    )(*parts)


def cut_kernel(spans, _, *refs):
    in_refs, out_refs = refs[:-spans], refs[-spans:]
    count = out_refs[0].shape[0]
    place = lax.axis_index("dp") & (spans - 1)
    for m, ref in enumerate(out_refs):
        rows = pl.ds((place ^ m) * count, count)
        total = in_refs[0][rows].astype(jnp.float32)
        for part in in_refs[1:]:
            total += part[rows].astype(jnp.float32)
        ref[...] = total.astype(ref.dtype)


def cut(before, parts, spans):
    shape = (parts[0].shape[0] // spans,) + parts[0].shape[1:]
    return pl.pallas_call(
        functools.partial(cut_kernel, spans),
        in_specs=[vmem()] * (1 + len(parts)),
        out_specs=[vmem()] * spans,
        out_shape=[jax.ShapeDtypeStruct(shape, jnp.float32)]
        + [jax.ShapeDtypeStruct(shape, jnp.bfloat16)] * (spans - 1),
        compiler_params=limit(before, *parts, *parts, *parts),
        name="cut",
    )(before, *parts)


def own_group(meta_ref, groups):
    return meta_ref[SECT] * (groups // 2) + meta_ref[DEPTH]


def merge_kernel(groups, meta_hbm, q_ref, o_ref, stat_ref, *refs):
    part_refs, out_refs = refs[: -groups - 3], refs[-groups - 3 : -3]
    held, meta_ref, sem = refs[-3:]
    fetch = pltpu.make_async_copy(meta_hbm, meta_ref, sem)
    fetch.start()
    count, steps, _ = q_ref.shape
    width = part_refs[0].shape[2] // 2
    rows = steps * GROUP
    fresh = part_refs[0][...]
    for ref in part_refs[1:]:
        fresh += ref[...].astype(jnp.float32)
    fresh = bf16(fresh).reshape(count * steps, 2 * width)
    shape = (count * rows, count * steps)
    row = lax.broadcasted_iota(jnp.int32, shape, 0)
    col = lax.broadcasted_iota(jnp.int32, shape, 1)
    causal = (row // rows == col // steps) & (col % steps <= row % steps)
    for kv in range(width // HEAD):
        q = jnp.concatenate([stacked_heads(q_ref[n], kv) for n in range(count)], axis=0)
        stat = jnp.concatenate([stat_ref[n, kv, :, :2] for n in range(count)], axis=0)
        o = jnp.concatenate([o_ref[n, kv] for n in range(count)], axis=0)
        k = fresh[:, kv * HEAD : (kv + 1) * HEAD]
        v = fresh[:, width + kv * HEAD : width + (kv + 1) * HEAD]
        s = jnp.where(causal, dot_t(q, k) * SCALE, -1e30)
        top = jnp.maximum(stat[:, :1], jnp.max(s, axis=1, keepdims=True))
        e = jnp.exp(s - top)
        back = jnp.exp(stat[:, :1] - top)
        share = 1.0 / (back * stat[:, 1:] + jnp.sum(e, axis=1, keepdims=True))
        r = bf16(o * (back * share) + dot32(bf16(e * share), v))
        for n in range(count):
            for g in range(GROUP):
                h = kv * GROUP + g
                first = n * rows + g * steps
                held[n, :, h * HEAD : (h + 1) * HEAD] = r[first : first + steps]
    fetch.wait()
    own = own_group(meta_ref, groups)
    slots = PROMPT + 2 * count
    step = lax.broadcasted_iota(jnp.int32, held.shape[1:], 0)
    for n in range(count):
        live = step < meta_ref[PROMPT + count + n]
        kept = jnp.where(live, held[n], jnp.zeros_like(held[n]))
        holder = lax.div(meta_ref[slots + own * count + n], count)
        for i in range(groups):

            @pl.when((holder ^ own) == i)
            def _():
                out_refs[i][...] = kept


def merge(meta, queries, o_cache, stats, parts, groups):
    shape = queries.shape[1:]
    return pl.pallas_call(
        functools.partial(merge_kernel, groups),
        in_specs=[pl.BlockSpec(memory_space=pl.ANY)] + [vmem()] * (3 + len(parts)),
        out_specs=[vmem()] * groups,
        out_shape=[jax.ShapeDtypeStruct(shape, jnp.bfloat16)] * groups,
        scratch_shapes=[
            pltpu.VMEM(queries.shape, jnp.bfloat16),
            pltpu.SMEM(meta.shape, jnp.int32),
            pltpu.SemaphoreType.DMA,
        ],
        compiler_params=limit(queries, o_cache, stats, *parts, *[queries] * (groups // queries.shape[0] + 1)),
        name="merge_fresh",
    )(meta, queries, o_cache, stats, *parts)


def pick_kernel(order, source_ref, *refs):
    in_refs, out_ref, held, sems = refs[:-3], refs[-3], refs[-2], refs[-1]
    count, _, width = held.shape
    stores = [pltpu.make_async_copy(held.at[r], out_ref.at[r], sems.at[r]) for r in range(count)]
    for r in range(count):
        source = source_ref[r]
        masks = [source == m for m in order[1:]]
        for first in range(0, width, HEAD):
            cols = slice(first, first + HEAD)
            row = in_refs[0][:, cols]
            for mask, ref in zip(masks, in_refs[1:]):
                row = jnp.where(mask, ref[:, cols], row)
            held[r, :, cols] = row
        stores[r].start()
    for store in stores:
        store.wait()


def pick(sources, blocks, order):
    out = jax.ShapeDtypeStruct(sources.shape[:1] + blocks[0].shape, jnp.bfloat16)
    return pl.pallas_call(
        functools.partial(pick_kernel, order),
        in_specs=[vmem()] * (1 + len(blocks)),
        out_specs=pl.BlockSpec(memory_space=pl.ANY),
        out_shape=out,
        scratch_shapes=[pltpu.VMEM(out.shape, out.dtype), pltpu.SemaphoreType.DMA(sources.shape[:1])],
        compiler_params=limit(sources, out, *blocks),
        name="pick_rows",
    )(sources, *blocks)


def shards(
    dp,
    w_key,
    w_value,
    hidden,
    queries,
    key_cache,
    value_cache,
    prompt_lengths,
    rollout_lengths,
    batch_slots,
):
    count, steps, feats = hidden.shape
    tokens = count * steps
    groups = 2 * dp
    spans = dp // 2
    wide = feats // dp
    x, z, t = lax.axis_index("sect"), lax.axis_index("dp"), lax.axis_index("tp")
    p, c = t >> 1, t & 1
    everyone = ("sect", "dp", "tp")
    devices = [(i, j, k) for i in range(2) for j in range(dp) for k in range(4)]

    def flat(i, j, k):
        return (i * dp + j) * 4 + k

    def send(a, target):
        return lax.ppermute(a, everyone, [(flat(*d), target(*d)) for d in devices])

    def to_features(m):
        def target(i, j, k):
            e, half = divmod(j ^ m, 2)
            return (k * spans + e) * 4 + half * 2 + i

        return target

    def to_mate(i, j, k):
        return flat(i, j, k ^ 1)

    def in_plane(m):
        return lambda i, j, k: flat(k & 1, j, ((k >> 1) ^ (m >> 1)) * 2 + (i ^ (m & 1)))

    def to_depth(m):
        return lambda i, j, k: flat(i, j ^ m, k)

    def to_group(m):
        return lambda i, j, k: ((i * dp + j) ^ m) * 4 + k

    scalars = jnp.stack([x, z]).astype(jnp.int32)
    meta = jnp.concatenate([scalars, prompt_lengths, rollout_lengths, batch_slots])

    flat_hidden = hidden.reshape(tokens, feats)
    near = [
        send(lax.dynamic_slice_in_dim(flat_hidden, (z ^ m) * wide, wide, 1), to_features(m))
        for m in range(dp)
    ]
    weights = (w_key, w_value)
    mates = [send(w, to_mate) for w in weights]
    o_cache, stats, sources = cache_attention(meta, queries, key_cache, value_cache, groups)

    parts = project(jnp.concatenate(near, axis=0), weights, mates, dp, steps)
    far, near = ([send(parts[first + m], in_plane(m)) for m in (3, 2, 1, 0)] for first in (0, 4))
    near = cut(stats, near + [send(add(far), to_depth(spans))], spans)
    parts = [a if m == 0 else send(a, to_depth(m)) for m, a in enumerate(near)]
    sends = merge(meta, queries, o_cache, stats, parts, groups)
    order = [dp] + sorted((m for m in range(1, groups) if m != dp), key=lambda m: -(m & (dp - 1)))
    blocks = [send(sends[m], to_group(m)) for m in order]
    return pick(sources, blocks + [sends[0]], order + [0])


def solution(mesh):
    in_specs = (
        P(("sect", "dp", "tp"), None),
        P(("sect", "dp", "tp"), None),
        P(("sect", "dp"), None, "tp"),
        P(("sect", "dp"), None, "tp"),
        P(("sect", "dp"), None, "tp"),
        P(("sect", "dp"), None, "tp"),
        P(("sect", "dp")),
        P(("sect", "dp")),
        P(),
    )
    out_specs = P(("sect", "dp"), None, "tp")
    body = functools.partial(shards, mesh.shape["dp"])
    return jax.shard_map(body, mesh=mesh, in_specs=in_specs, out_specs=out_specs, check_vma=False)
```

```python
import functools
import jax
import jax.numpy as jnp
from jax import lax
from jax.experimental import pallas as pl
from jax.experimental.pallas import tpu as pltpu
from jax.sharding import PartitionSpec as P

HEAD = 128
GROUP = 8
SCALE = HEAD ** (-0.5)
MIB = 1 << 20
SECT, DEPTH, PROMPT = range(3)


def vmem():
    return pl.BlockSpec(memory_space=pltpu.VMEM)


def smem():
    return pl.BlockSpec(memory_space=pltpu.SMEM)


def limit(*arrays):
    total = sum(a.size * a.dtype.itemsize for a in arrays)
    return pltpu.CompilerParams(vmem_limit_bytes=max(6 * MIB, total + 2 * MIB))


def stacked_heads(q, kv):
    first = kv * GROUP
    return jnp.concatenate(
        [q[:, (first + g) * HEAD : (first + g + 1) * HEAD] for g in range(GROUP)], axis=0
    )


def dot32(a, b):
    return jnp.dot(a, b, preferred_element_type=jnp.float32)


def dot_t(a, b):
    return lax.dot_general(a, b, (((1,), (1,)), ((), ())), preferred_element_type=jnp.float32)


def bf16(a):
    return a.astype(jnp.bfloat16)


def cache_kernel(groups, meta_ref, q_ref, k_ref, v_ref, o_ref, stat_ref, source_ref, places):
    count = source_ref.shape[0]

    @pl.when(pl.program_id(0) == 0)
    def _():
        def note(s, carry):
            places[meta_ref[PROMPT + 2 * count + s]] = s
            return carry

        lax.fori_loop(0, groups * count, note, 0, unroll=8)
        own = own_group(meta_ref, groups)
        for r in range(count):
            source = lax.div(places[own * count + r], count) ^ own
            source_ref[r] = bf16(jnp.full(source_ref.shape[1:], source.astype(jnp.float32)))

    slots, width = k_ref.shape[1:]
    steps = q_ref.shape[1]
    rows = steps * GROUP
    live = lax.broadcasted_iota(jnp.int32, (rows, slots), 1) < meta_ref[PROMPT + pl.program_id(0)]
    lane = lax.broadcasted_iota(jnp.int32, (rows, HEAD), 1)
    for kv in range(width // HEAD):
        cols = slice(kv * HEAD, (kv + 1) * HEAD)
        q = stacked_heads(q_ref[0], kv)
        s = jnp.where(live, dot_t(q, k_ref[0, :, cols]) * SCALE, -1e30)
        top = jnp.max(s, axis=1, keepdims=True)
        e = jnp.exp(s - top)
        total = jnp.sum(e, axis=1, keepdims=True)
        o_ref[0, kv] = dot32(bf16(e), v_ref[0, :, cols])
        stat_ref[0, kv] = jnp.where(lane == 0, top, total)


def cache_attention(meta, queries, key_cache, value_cache, groups):
    count, steps, qw = queries.shape
    slots, width = key_cache.shape[1:]
    shape = (count, width // HEAD, steps * GROUP, HEAD)

    def one(n, meta):
        return (n, 0, 0)

    def one4(n, meta):
        return (n, 0, 0, 0)

    return pl.pallas_call(
        functools.partial(cache_kernel, groups),
        grid_spec=pltpu.PrefetchScalarGridSpec(
            num_scalar_prefetch=1,
            grid=(count,),
            in_specs=[
                pl.BlockSpec((1, steps, qw), one),
                pl.BlockSpec((1, slots, width), one),
                pl.BlockSpec((1, slots, width), one),
            ],
            out_specs=[pl.BlockSpec((1,) + shape[1:], one4)] * 2
            + [pl.BlockSpec((count, steps, HEAD), lambda n, meta: (0, 0, 0))],
            scratch_shapes=[pltpu.SMEM((groups * count,), jnp.int32)],
        ),
        out_shape=[jax.ShapeDtypeStruct(shape, jnp.float32)] * 2
        + [jax.ShapeDtypeStruct((count, steps, HEAD), jnp.bfloat16)],
        compiler_params=pltpu.CompilerParams(vmem_limit_bytes=8 * MIB),
        name="cache_attention",
    )(meta, queries, key_cache, value_cache)


def project_kernel(dp, x_ref, key_ref, value_ref, key_mate_ref, value_mate_ref, *refs):
    out_refs, held = refs[:8], refs[8]
    seqs, steps, width = held.shape
    count = seqs // dp
    rows, kind_width = key_ref.shape
    core, half = lax.axis_index("tp") & 1, lax.axis_index("tp") >> 1
    sect, depth = lax.axis_index("sect"), lax.axis_index("dp")
    first, second = x_ref[:, :rows], x_ref[:, rows:]
    own, mate = jnp.where(core == 0, first, second), jnp.where(core == 0, second, first)
    place = (depth & (dp // 2 - 1)) * 2 + half
    chunk = 4 * count * steps
    for kind, refs in enumerate(((key_ref, key_mate_ref), (value_ref, value_mate_ref))):
        cols = slice(kind * kind_width, (kind + 1) * kind_width)
        for m in range(dp):
            if m % 4 == 0:
                part = slice(m * count * steps, m * count * steps + chunk)
                sums = bf16(dot32(own[part], refs[0][...]) + dot32(mate[part], refs[1][...]))
            for n in range(count):
                i = (m % 4) * count + n
                held[(place ^ m) * count + n, :, cols] = sums[i * steps : (i + 1) * steps]
    cw = width // 8
    own_half = (depth >= dp // 2).astype(jnp.int32)
    for i, ref in enumerate(out_refs):
        t = (half ^ ((i >> 1) & 1)) * 2 + (sect ^ (i & 1))
        group = pl.ds((own_half ^ (1 - (i >> 2))) * (seqs // 2), seqs // 2)
        for kind in range(2):
            cols = pl.ds(pl.multiple_of(kind * kind_width + t * cw, cw), cw)
            ref[:, :, kind * cw : (kind + 1) * cw] = held[group, :, cols]


def project(x, weights, mates, dp, steps):
    seqs = x.shape[0] // steps
    rows, width = weights[0].shape
    out = jax.ShapeDtypeStruct((seqs // 2, steps, width // 2), jnp.bfloat16)
    return pl.pallas_call(
        functools.partial(project_kernel, dp),
        in_specs=[vmem()] * 5,
        out_specs=[vmem()] * 8,
        out_shape=[out] * 8,
        scratch_shapes=[pltpu.VMEM((seqs, steps, 2 * width), jnp.bfloat16)],
        compiler_params=limit(x, *weights, *weights, *weights, *weights, *[out] * 32),
        name="project",
    )(x, *weights, *mates)


def add_kernel(*refs):
    total = refs[0][...].astype(jnp.float32)
    for ref in refs[1:-1]:
        total += ref[...].astype(jnp.float32)
    refs[-1][...] = bf16(total)


def add(parts):
    out = jax.ShapeDtypeStruct(parts[0].shape, jnp.bfloat16)
    return pl.pallas_call(
        add_kernel,
        in_specs=[vmem()] * len(parts),
        out_specs=vmem(),
        out_shape=out,
        compiler_params=limit(out, out, out, *parts),
        name="add",
    )(*parts)


def cut_kernel(spans, _, *refs):
    in_refs, out_refs = refs[:-spans], refs[-spans:]
    count = out_refs[0].shape[0]
    place = lax.axis_index("dp") & (spans - 1)
    for m, ref in enumerate(out_refs):
        rows = pl.ds((place ^ m) * count, count)
        total = in_refs[0][rows].astype(jnp.float32)
        for part in in_refs[1:]:
            total += part[rows].astype(jnp.float32)
        ref[...] = total.astype(ref.dtype)


def cut(before, parts, spans):
    shape = (parts[0].shape[0] // spans,) + parts[0].shape[1:]
    return pl.pallas_call(
        functools.partial(cut_kernel, spans),
        in_specs=[vmem()] * (1 + len(parts)),
        out_specs=[vmem()] * spans,
        out_shape=[jax.ShapeDtypeStruct(shape, jnp.float32)]
        + [jax.ShapeDtypeStruct(shape, jnp.bfloat16)] * (spans - 1),
        compiler_params=limit(before, *parts, *parts, *parts),
        name="cut",
    )(before, *parts)


def own_group(meta_ref, groups):
    return meta_ref[SECT] * (groups // 2) + meta_ref[DEPTH]


def merge_kernel(groups, meta_hbm, q_ref, o_ref, stat_ref, *refs):
    part_refs, out_refs = refs[: -groups - 3], refs[-groups - 3 : -3]
    held, meta_ref, sem = refs[-3:]
    fetch = pltpu.make_async_copy(meta_hbm, meta_ref, sem)
    fetch.start()
    count, steps, _ = q_ref.shape
    width = part_refs[0].shape[2] // 2
    rows = steps * GROUP
    fresh = part_refs[0][...]
    for ref in part_refs[1:]:
        fresh += ref[...].astype(jnp.float32)
    fresh = bf16(fresh).reshape(count * steps, 2 * width)
    shape = (count * rows, count * steps)
    row = lax.broadcasted_iota(jnp.int32, shape, 0)
    col = lax.broadcasted_iota(jnp.int32, shape, 1)
    causal = (row // rows == col // steps) & (col % steps <= row % steps)
    for kv in range(width // HEAD):
        q = jnp.concatenate([stacked_heads(q_ref[n], kv) for n in range(count)], axis=0)
        stat = jnp.concatenate([stat_ref[n, kv, :, :2] for n in range(count)], axis=0)
        o = jnp.concatenate([o_ref[n, kv] for n in range(count)], axis=0)
        k = fresh[:, kv * HEAD : (kv + 1) * HEAD]
        v = fresh[:, width + kv * HEAD : width + (kv + 1) * HEAD]
        s = jnp.where(causal, dot_t(q, k) * SCALE, -1e30)
        top = jnp.maximum(stat[:, :1], jnp.max(s, axis=1, keepdims=True))
        e = jnp.exp(s - top)
        back = jnp.exp(stat[:, :1] - top)
        share = 1.0 / (back * stat[:, 1:] + jnp.sum(e, axis=1, keepdims=True))
        r = bf16(o * (back * share) + dot32(bf16(e * share), v))
        for n in range(count):
            for g in range(GROUP):
                h = kv * GROUP + g
                first = n * rows + g * steps
                held[n, :, h * HEAD : (h + 1) * HEAD] = r[first : first + steps]
    fetch.wait()
    own = own_group(meta_ref, groups)
    slots = PROMPT + 2 * count
    step = lax.broadcasted_iota(jnp.int32, held.shape[1:], 0)
    for n in range(count):
        live = step < meta_ref[PROMPT + count + n]
        kept = jnp.where(live, held[n], jnp.zeros_like(held[n]))
        holder = lax.div(meta_ref[slots + own * count + n], count)
        for i in range(groups):

            @pl.when((holder ^ own) == i)
            def _():
                out_refs[i][...] = kept


def merge(meta, queries, o_cache, stats, parts, groups):
    shape = queries.shape[1:]
    return pl.pallas_call(
        functools.partial(merge_kernel, groups),
        in_specs=[pl.BlockSpec(memory_space=pl.ANY)] + [vmem()] * (3 + len(parts)),
        out_specs=[vmem()] * groups,
        out_shape=[jax.ShapeDtypeStruct(shape, jnp.bfloat16)] * groups,
        scratch_shapes=[
            pltpu.VMEM(queries.shape, jnp.bfloat16),
            pltpu.SMEM(meta.shape, jnp.int32),
            pltpu.SemaphoreType.DMA,
        ],
        compiler_params=limit(queries, o_cache, stats, *parts, *[queries] * (groups // queries.shape[0] + 1)),
        name="merge_fresh",
    )(meta, queries, o_cache, stats, *parts)


def pick_kernel(order, source_ref, *refs):
    in_refs, out_ref, held, sems = refs[:-3], refs[-3], refs[-2], refs[-1]
    count, _, width = held.shape
    stores = [pltpu.make_async_copy(held.at[r], out_ref.at[r], sems.at[r]) for r in range(count)]
    for r in range(count):
        source = source_ref[r]
        masks = [source == m for m in order[1:]]
        for first in range(0, width, HEAD):
            cols = slice(first, first + HEAD)
            row = in_refs[0][:, cols]
            for mask, ref in zip(masks, in_refs[1:]):
                row = jnp.where(mask, ref[:, cols], row)
            held[r, :, cols] = row
        stores[r].start()
    for store in stores:
        store.wait()


def pick(sources, blocks, order):
    out = jax.ShapeDtypeStruct(sources.shape[:1] + blocks[0].shape, jnp.bfloat16)
    return pl.pallas_call(
        functools.partial(pick_kernel, order),
        in_specs=[vmem()] * (1 + len(blocks)),
        out_specs=pl.BlockSpec(memory_space=pl.ANY),
        out_shape=out,
        scratch_shapes=[pltpu.VMEM(out.shape, out.dtype), pltpu.SemaphoreType.DMA(sources.shape[:1])],
        compiler_params=limit(sources, out, *blocks),
        name="pick_rows",
    )(sources, *blocks)


def shards(
    dp,
    w_key,
    w_value,
    hidden,
    queries,
    key_cache,
    value_cache,
    prompt_lengths,
    rollout_lengths,
    batch_slots,
):
    count, steps, feats = hidden.shape
    tokens = count * steps
    groups = 2 * dp
    spans = dp // 2
    wide = feats // dp
    x, z, t = lax.axis_index("sect"), lax.axis_index("dp"), lax.axis_index("tp")
    p, c = t >> 1, t & 1
    everyone = ("sect", "dp", "tp")
    devices = [(i, j, k) for i in range(2) for j in range(dp) for k in range(4)]

    def flat(i, j, k):
        return (i * dp + j) * 4 + k

    def send(a, target):
        return lax.ppermute(a, everyone, [(flat(*d), target(*d)) for d in devices])

    def to_features(m):
        def target(i, j, k):
            e, half = divmod(j ^ m, 2)
            return (k * spans + e) * 4 + half * 2 + i

        return target

    def to_mate(i, j, k):
        return flat(i, j, k ^ 1)

    def in_plane(m):
        return lambda i, j, k: flat(k & 1, j, ((k >> 1) ^ (m >> 1)) * 2 + (i ^ (m & 1)))

    def to_depth(m):
        return lambda i, j, k: flat(i, j ^ m, k)

    def to_group(m):
        return lambda i, j, k: ((i * dp + j) ^ m) * 4 + k

    scalars = jnp.stack([x, z]).astype(jnp.int32)
    meta = jnp.concatenate([scalars, prompt_lengths, rollout_lengths, batch_slots])

    flat_hidden = hidden.reshape(tokens, feats)
    near = []
    for m in range(dp):
        piece = lax.dynamic_slice_in_dim(flat_hidden, (z ^ m) * wide, wide, 1)
        flat_hidden, piece = lax.optimization_barrier((flat_hidden, piece))
        near.append(send(piece, to_features(m)))
    weights = (w_key, w_value)
    mates = [send(w, to_mate) for w in weights]
    o_cache, stats, sources = cache_attention(meta, queries, key_cache, value_cache, groups)

    parts = project(jnp.concatenate(near, axis=0), weights, mates, dp, steps)
    far, near = ([send(parts[first + m], in_plane(m)) for m in (3, 2, 1, 0)] for first in (0, 4))
    near = cut(stats, near + [send(add(far), to_depth(spans))], spans)
    parts = [a if m == 0 else send(a, to_depth(m)) for m, a in enumerate(near)]
    sends = merge(meta, queries, o_cache, stats, parts, groups)
    order = sorted(range(1, groups), key=lambda m: -(m & (dp - 1)))
    blocks = [send(sends[m], to_group(m)) for m in order]
    return pick(sources, blocks + [sends[0]], order + [0])


def solution(mesh):
    in_specs = (
        P(("sect", "dp", "tp"), None),
        P(("sect", "dp", "tp"), None),
        P(("sect", "dp"), None, "tp"),
        P(("sect", "dp"), None, "tp"),
        P(("sect", "dp"), None, "tp"),
        P(("sect", "dp"), None, "tp"),
        P(("sect", "dp")),
        P(("sect", "dp")),
        P(),
    )
    out_specs = P(("sect", "dp"), None, "tp")
    body = functools.partial(shards, mesh.shape["dp"])
    return jax.shard_map(body, mesh=mesh, in_specs=in_specs, out_specs=out_specs, check_vma=False)
```

```python
import functools
import jax
import jax.numpy as jnp
from jax import lax
from jax.experimental import pallas as pl
from jax.experimental.pallas import tpu as pltpu
from jax.sharding import PartitionSpec as P

HEAD = 128
GROUP = 8
SCALE = HEAD ** (-0.5)
MIB = 1 << 20
SECT, DEPTH, PROMPT = range(3)


def vmem():
    return pl.BlockSpec(memory_space=pltpu.VMEM)


def smem():
    return pl.BlockSpec(memory_space=pltpu.SMEM)


def limit(*arrays):
    total = sum(a.size * a.dtype.itemsize for a in arrays)
    return pltpu.CompilerParams(vmem_limit_bytes=max(6 * MIB, total + 2 * MIB))


def stacked_heads(q, kv):
    first = kv * GROUP
    return jnp.concatenate(
        [q[:, (first + g) * HEAD : (first + g + 1) * HEAD] for g in range(GROUP)], axis=0
    )


def dot32(a, b):
    return jnp.dot(a, b, preferred_element_type=jnp.float32)


def dot_t(a, b):
    return lax.dot_general(a, b, (((1,), (1,)), ((), ())), preferred_element_type=jnp.float32)


def bf16(a):
    return a.astype(jnp.bfloat16)


def cache_kernel(groups, meta_ref, q_ref, k_ref, v_ref, o_ref, stat_ref, source_ref, places):
    count = source_ref.shape[0]

    @pl.when(pl.program_id(0) == 0)
    def _():
        def note(s, carry):
            places[meta_ref[PROMPT + 2 * count + s]] = s
            return carry

        lax.fori_loop(0, groups * count, note, 0, unroll=8)
        own = own_group(meta_ref, groups)
        for r in range(count):
            source = lax.div(places[own * count + r], count) ^ own
            source_ref[r] = bf16(jnp.full(source_ref.shape[1:], source.astype(jnp.float32)))

    slots, width = k_ref.shape[1:]
    steps = q_ref.shape[1]
    rows = steps * GROUP
    live = lax.broadcasted_iota(jnp.int32, (rows, slots), 1) < meta_ref[PROMPT + pl.program_id(0)]
    lane = lax.broadcasted_iota(jnp.int32, (rows, HEAD), 1)
    for kv in range(width // HEAD):
        cols = slice(kv * HEAD, (kv + 1) * HEAD)
        q = stacked_heads(q_ref[0], kv)
        s = jnp.where(live, dot_t(q, k_ref[0, :, cols]) * SCALE, -1e30)
        top = jnp.max(s, axis=1, keepdims=True)
        e = jnp.exp(s - top)
        total = jnp.sum(e, axis=1, keepdims=True)
        o_ref[0, kv] = dot32(bf16(e), v_ref[0, :, cols])
        stat_ref[0, kv] = jnp.where(lane == 0, top, total)


def cache_attention(meta, queries, key_cache, value_cache, groups):
    count, steps, qw = queries.shape
    slots, width = key_cache.shape[1:]
    shape = (count, width // HEAD, steps * GROUP, HEAD)

    def one(n, meta):
        return (n, 0, 0)

    def one4(n, meta):
        return (n, 0, 0, 0)

    return pl.pallas_call(
        functools.partial(cache_kernel, groups),
        grid_spec=pltpu.PrefetchScalarGridSpec(
            num_scalar_prefetch=1,
            grid=(count,),
            in_specs=[
                pl.BlockSpec((1, steps, qw), one),
                pl.BlockSpec((1, slots, width), one),
                pl.BlockSpec((1, slots, width), one),
            ],
            out_specs=[pl.BlockSpec((1,) + shape[1:], one4)] * 2
            + [pl.BlockSpec((count, steps, HEAD), lambda n, meta: (0, 0, 0))],
            scratch_shapes=[pltpu.SMEM((groups * count,), jnp.int32)],
        ),
        out_shape=[jax.ShapeDtypeStruct(shape, jnp.float32)] * 2
        + [jax.ShapeDtypeStruct((count, steps, HEAD), jnp.bfloat16)],
        compiler_params=pltpu.CompilerParams(vmem_limit_bytes=8 * MIB),
        name="cache_attention",
    )(meta, queries, key_cache, value_cache)


def project_kernel(dp, x_ref, key_ref, value_ref, key_mate_ref, value_mate_ref, *refs):
    out_refs, held = refs[:8], refs[8]
    seqs, steps, width = held.shape
    count = seqs // dp
    rows, kind_width = key_ref.shape
    core, half = lax.axis_index("tp") & 1, lax.axis_index("tp") >> 1
    sect, depth = lax.axis_index("sect"), lax.axis_index("dp")
    first, second = x_ref[:, :rows], x_ref[:, rows:]
    own, mate = jnp.where(core == 0, first, second), jnp.where(core == 0, second, first)
    place = (depth & (dp // 2 - 1)) * 2 + half
    chunk = 4 * count * steps
    for kind, refs in enumerate(((key_ref, key_mate_ref), (value_ref, value_mate_ref))):
        cols = slice(kind * kind_width, (kind + 1) * kind_width)
        for m in range(dp):
            if m % 4 == 0:
                part = slice(m * count * steps, m * count * steps + chunk)
                sums = bf16(dot32(own[part], refs[0][...]) + dot32(mate[part], refs[1][...]))
            for n in range(count):
                i = (m % 4) * count + n
                held[(place ^ m) * count + n, :, cols] = sums[i * steps : (i + 1) * steps]
    cw = width // 8
    own_half = (depth >= dp // 2).astype(jnp.int32)
    for i, ref in enumerate(out_refs):
        t = (half ^ ((i >> 1) & 1)) * 2 + (sect ^ (i & 1))
        group = pl.ds((own_half ^ (1 - (i >> 2))) * (seqs // 2), seqs // 2)
        for kind in range(2):
            cols = pl.ds(pl.multiple_of(kind * kind_width + t * cw, cw), cw)
            ref[:, :, kind * cw : (kind + 1) * cw] = held[group, :, cols]


def project(x, weights, mates, dp, steps):
    seqs = x.shape[0] // steps
    rows, width = weights[0].shape
    out = jax.ShapeDtypeStruct((seqs // 2, steps, width // 2), jnp.bfloat16)
    return pl.pallas_call(
        functools.partial(project_kernel, dp),
        in_specs=[vmem()] * 5,
        out_specs=[vmem()] * 8,
        out_shape=[out] * 8,
        scratch_shapes=[pltpu.VMEM((seqs, steps, 2 * width), jnp.bfloat16)],
        compiler_params=limit(x, *weights, *weights, *weights, *weights, *[out] * 32),
        name="project",
    )(x, *weights, *mates)


def add_kernel(*refs):
    total = refs[0][...].astype(jnp.float32)
    for ref in refs[1:-1]:
        total += ref[...].astype(jnp.float32)
    refs[-1][...] = bf16(total)


def add(parts):
    out = jax.ShapeDtypeStruct(parts[0].shape, jnp.bfloat16)
    return pl.pallas_call(
        add_kernel,
        in_specs=[vmem()] * len(parts),
        out_specs=vmem(),
        out_shape=out,
        compiler_params=limit(out, out, out, *parts),
        name="add",
    )(*parts)


def cut_kernel(spans, _, *refs):
    in_refs, out_refs = refs[:-spans], refs[-spans:]
    count = out_refs[0].shape[0]
    place = lax.axis_index("dp") & (spans - 1)
    for m, ref in enumerate(out_refs):
        rows = pl.ds((place ^ m) * count, count)
        total = in_refs[0][rows].astype(jnp.float32)
        for part in in_refs[1:]:
            total += part[rows].astype(jnp.float32)
        ref[...] = total.astype(ref.dtype)


def cut(before, parts, spans):
    shape = (parts[0].shape[0] // spans,) + parts[0].shape[1:]
    return pl.pallas_call(
        functools.partial(cut_kernel, spans),
        in_specs=[vmem()] * (1 + len(parts)),
        out_specs=[vmem()] * spans,
        out_shape=[jax.ShapeDtypeStruct(shape, jnp.float32)]
        + [jax.ShapeDtypeStruct(shape, jnp.bfloat16)] * (spans - 1),
        compiler_params=limit(before, *parts, *parts, *parts),
        name="cut",
    )(before, *parts)


def own_group(meta_ref, groups):
    return meta_ref[SECT] * (groups // 2) + meta_ref[DEPTH]


def merge_kernel(groups, meta_hbm, q_ref, o_ref, stat_ref, *refs):
    part_refs, out_refs = refs[: -groups - 3], refs[-groups - 3 : -3]
    held, meta_ref, sem = refs[-3:]
    fetch = pltpu.make_async_copy(meta_hbm, meta_ref, sem)
    fetch.start()
    count, steps, _ = q_ref.shape
    width = part_refs[0].shape[2] // 2
    rows = steps * GROUP
    fresh = part_refs[0][...]
    for ref in part_refs[1:]:
        fresh += ref[...].astype(jnp.float32)
    fresh = bf16(fresh).reshape(count * steps, 2 * width)
    shape = (count * rows, count * steps)
    row = lax.broadcasted_iota(jnp.int32, shape, 0)
    col = lax.broadcasted_iota(jnp.int32, shape, 1)
    causal = (row // rows == col // steps) & (col % steps <= row % steps)
    for kv in range(width // HEAD):
        q = jnp.concatenate([stacked_heads(q_ref[n], kv) for n in range(count)], axis=0)
        stat = jnp.concatenate([stat_ref[n, kv, :, :2] for n in range(count)], axis=0)
        o = jnp.concatenate([o_ref[n, kv] for n in range(count)], axis=0)
        k = fresh[:, kv * HEAD : (kv + 1) * HEAD]
        v = fresh[:, width + kv * HEAD : width + (kv + 1) * HEAD]
        s = jnp.where(causal, dot_t(q, k) * SCALE, -1e30)
        top = jnp.maximum(stat[:, :1], jnp.max(s, axis=1, keepdims=True))
        e = jnp.exp(s - top)
        back = jnp.exp(stat[:, :1] - top)
        share = 1.0 / (back * stat[:, 1:] + jnp.sum(e, axis=1, keepdims=True))
        r = bf16(o * (back * share) + dot32(bf16(e * share), v))
        for n in range(count):
            for g in range(GROUP):
                h = kv * GROUP + g
                first = n * rows + g * steps
                held[n, :, h * HEAD : (h + 1) * HEAD] = r[first : first + steps]
    fetch.wait()
    own = own_group(meta_ref, groups)
    slots = PROMPT + 2 * count
    step = lax.broadcasted_iota(jnp.int32, held.shape[1:], 0)
    for n in range(count):
        live = step < meta_ref[PROMPT + count + n]
        kept = jnp.where(live, held[n], jnp.zeros_like(held[n]))
        holder = lax.div(meta_ref[slots + own * count + n], count)
        for i in range(groups):

            @pl.when((holder ^ own) == i)
            def _():
                out_refs[i][...] = kept


def merge(meta, queries, o_cache, stats, parts, groups):
    shape = queries.shape[1:]
    return pl.pallas_call(
        functools.partial(merge_kernel, groups),
        in_specs=[pl.BlockSpec(memory_space=pl.ANY)] + [vmem()] * (3 + len(parts)),
        out_specs=[vmem()] * groups,
        out_shape=[jax.ShapeDtypeStruct(shape, jnp.bfloat16)] * groups,
        scratch_shapes=[
            pltpu.VMEM(queries.shape, jnp.bfloat16),
            pltpu.SMEM(meta.shape, jnp.int32),
            pltpu.SemaphoreType.DMA,
        ],
        compiler_params=limit(queries, o_cache, stats, *parts, *[queries] * (groups // queries.shape[0] + 1)),
        name="merge_fresh",
    )(meta, queries, o_cache, stats, *parts)


def pick_kernel(order, source_ref, *refs):
    in_refs, out_ref, held, sems = refs[:-3], refs[-3], refs[-2], refs[-1]
    count, _, width = held.shape
    stores = [pltpu.make_async_copy(held.at[r], out_ref.at[r], sems.at[r]) for r in range(count)]
    for r in range(count):
        source = source_ref[r]
        masks = [source == m for m in order[1:]]
        for first in range(0, width, HEAD):
            cols = slice(first, first + HEAD)
            row = in_refs[0][:, cols]
            for mask, ref in zip(masks, in_refs[1:]):
                row = jnp.where(mask, ref[:, cols], row)
            held[r, :, cols] = row
        stores[r].start()
    for store in stores:
        store.wait()


def pick(sources, blocks, order):
    out = jax.ShapeDtypeStruct(sources.shape[:1] + blocks[0].shape, jnp.bfloat16)
    return pl.pallas_call(
        functools.partial(pick_kernel, order),
        in_specs=[vmem()] * (1 + len(blocks)),
        out_specs=pl.BlockSpec(memory_space=pl.ANY),
        out_shape=out,
        scratch_shapes=[pltpu.VMEM(out.shape, out.dtype), pltpu.SemaphoreType.DMA(sources.shape[:1])],
        compiler_params=limit(sources, out, *blocks),
        name="pick_rows",
    )(sources, *blocks)


def shards(
    dp,
    w_key,
    w_value,
    hidden,
    queries,
    key_cache,
    value_cache,
    prompt_lengths,
    rollout_lengths,
    batch_slots,
):
    count, steps, feats = hidden.shape
    tokens = count * steps
    groups = 2 * dp
    spans = dp // 2
    wide = feats // dp
    x, z, t = lax.axis_index("sect"), lax.axis_index("dp"), lax.axis_index("tp")
    p, c = t >> 1, t & 1
    everyone = ("sect", "dp", "tp")
    devices = [(i, j, k) for i in range(2) for j in range(dp) for k in range(4)]

    def flat(i, j, k):
        return (i * dp + j) * 4 + k

    def send(a, target):
        return lax.ppermute(a, everyone, [(flat(*d), target(*d)) for d in devices])

    def to_features(m):
        def target(i, j, k):
            e, half = divmod(j ^ m, 2)
            return (k * spans + e) * 4 + half * 2 + i

        return target

    def to_mate(i, j, k):
        return flat(i, j, k ^ 1)

    def in_plane(m):
        return lambda i, j, k: flat(k & 1, j, ((k >> 1) ^ (m >> 1)) * 2 + (i ^ (m & 1)))

    def to_depth(m):
        return lambda i, j, k: flat(i, j ^ m, k)

    def to_group(m):
        return lambda i, j, k: ((i * dp + j) ^ m) * 4 + k

    scalars = jnp.stack([x, z]).astype(jnp.int32)
    meta = jnp.concatenate([scalars, prompt_lengths, rollout_lengths, batch_slots])

    flat_hidden = hidden.reshape(tokens, feats)
    near = [
        send(lax.dynamic_slice_in_dim(flat_hidden, (z ^ m) * wide, wide, 1), to_features(m))
        for m in range(dp)
    ]
    weights = (w_key, w_value)
    mates = [send(w, to_mate) for w in weights]
    o_cache, stats, sources = cache_attention(meta, queries, key_cache, value_cache, groups)

    parts = project(jnp.concatenate(near, axis=0), weights, mates, dp, steps)
    far, near = ([send(parts[first + m], in_plane(m)) for m in (3, 2, 1, 0)] for first in (0, 4))
    near = cut(stats, near + [send(add(far), to_depth(spans))], spans)
    parts = [a if m == 0 else send(a, to_depth(m)) for m, a in enumerate(near)]
    sends = merge(meta, queries, o_cache, stats, parts, groups)
    order = sorted(range(1, groups), key=lambda m: (-(m & (dp - 1)), -m))
    blocks = [send(sends[m], to_group(m)) for m in order]
    return pick(sources, blocks + [sends[0]], order + [0])


def solution(mesh):
    in_specs = (
        P(("sect", "dp", "tp"), None),
        P(("sect", "dp", "tp"), None),
        P(("sect", "dp"), None, "tp"),
        P(("sect", "dp"), None, "tp"),
        P(("sect", "dp"), None, "tp"),
        P(("sect", "dp"), None, "tp"),
        P(("sect", "dp")),
        P(("sect", "dp")),
        P(),
    )
    out_specs = P(("sect", "dp"), None, "tp")
    body = functools.partial(shards, mesh.shape["dp"])
    return jax.shard_map(body, mesh=mesh, in_specs=in_specs, out_specs=out_specs, check_vma=False)
```
